32 devices in a mesh: tok: 4 (over y, x), blk: 8 (over z, core).
Axes of the slice: x: 2, y: 2, z: 4, core: 2. Of those that a mesh axis runs over, the one named last changes fastest.
Arguments:
- features: bfloat16 [2048, 8192], P('tok'), may hold values from -6 to 6
- hidden_grad: bfloat16 [2048, 28672], P('tok', 'blk'), may hold values from -0.125 to 0.125
- block_mask: int32 [64, 224], replicated, may hold values from 0 to 1, as said below
- old_columns: int32 [8, 28], replicated, may hold values from 0 to 224, as said below
- new_columns: int32 [8, 28], replicated, may hold values from 0 to 224, as said below
- weights: float32 [4, 224, 8, 128, 128], P('tok', 'blk'), may hold values from -0.75 to 0.75
- first_moment: float32 [4, 224, 8, 128, 128], P('tok', 'blk'), may hold values from -6 to 6
- second_moment: float32 [4, 224, 8, 128, 128], P('tok', 'blk'), may hold values from 0.001 to 1
Outputs:
- new_weights: float32 [4, 224, 8, 128, 128], P('tok', 'blk')
- new_first: float32 [4, 224, 8, 128, 128], P('tok', 'blk')
- new_second: float32 [4, 224, 8, 128, 128], P('tok', 'blk')
The draws below stay inside these ranges and needn't reach their ends.
Inputs may be any that keep to these rules, and one draw needn't show every extreme that they name: `block_mask`: in every column, each aligned group of 16 row blocks holds at most 8 ones; some group holds exactly 8. `old_columns`: every column number below 224 stands exactly once; all other entries are 224. `new_columns`: equal to old_columns except that, for some owners k, the entries [k, 0] and [(k + 1) mod 8, 27] of old_columns are exchanged.
All inputs are finite; a program needn't handle non-finite values.
Results may differ from the reference program's by a relative error of at most 0.0003.
Values may be sent and summed in bfloat16 or wider, within the bound.
A program may use at most 448 MiB of HBM per device.

```python
import math
import jax
import jax.numpy as jnp
from jax import lax

D = 8192
BS = 128
NRB = 64
NCB = 224
RB_T = 16
KCAP = 8
OWNERS = 8
CSLOT = 28
SLOTS_ALL = 224
TOKENS = 2048
N_TOK = 4


def draw_pattern(key):
    mask_key = jax.random.fold_in(key, 11)
    count_key, score_key, row_key, col_key = jax.random.split(mask_key, 4)
    ranges = NRB // RB_T
    counts = jax.random.randint(count_key, (ranges, NCB), 0, KCAP + 1)
    home_range = jnp.arange(ranges)[:, None] == jnp.arange(NCB)[None, :] % ranges
    counts = jnp.where(home_range, jnp.maximum(counts, 1), counts)
    pick_range = jax.random.randint(row_key, (), 0, ranges)
    pick_column = jax.random.randint(col_key, (), 0, NCB)
    forced = (jnp.arange(ranges)[:, None] == pick_range) & (jnp.arange(NCB)[None, :] == pick_column)
    counts = jnp.where(forced, KCAP, counts)
    scores = jax.random.randint(score_key, (ranges, NCB, RB_T), 0, 1 << 20) * RB_T + jnp.arange(RB_T)[None, None, :]
    rank_of = jnp.argsort(jnp.argsort(scores, axis=2), axis=2)
    filled = (rank_of < counts[:, :, None]).astype(jnp.int32)
    return jnp.transpose(filled, (0, 2, 1)).reshape(NRB, NCB).astype(jnp.int32)


def draw_owners(key):
    pattern = draw_pattern(key)
    owners = jnp.arange(OWNERS)
    forced_owner = (owners == 0) | (owners == OWNERS - 1) | (owners == OWNERS // 2) | (owners == OWNERS // 2 - 1)
    slot_owner = jnp.arange(SLOTS_ALL) // CSLOT
    slot_pos = jnp.arange(SLOTS_ALL) % CSLOT
    forced_slot = forced_owner[slot_owner] & (slot_pos == 0) | forced_owner[(slot_owner + OWNERS - 1) % OWNERS] & (slot_pos == CSLOT - 1)
    scores = jax.random.randint(jax.random.fold_in(key, 31), (SLOTS_ALL,), 0, 1 << 16) * SLOTS_ALL + jnp.arange(SLOTS_ALL)
    priority = scores + jnp.where(forced_slot, 0, (1 << 16) * SLOTS_ALL)
    order = jnp.argsort(priority)
    id_sequence = jnp.concatenate([jax.random.permutation(jax.random.fold_in(key, 23), NCB), jnp.arange(NCB, SLOTS_ALL)]).astype(jnp.int32)
    old_flat = jnp.zeros((SLOTS_ALL,), jnp.int32).at[order].set(id_sequence)
    old_slots = jnp.where(old_flat < NCB, old_flat, NCB).astype(jnp.int32).reshape(OWNERS, CSLOT)
    per_column = jnp.concatenate([jnp.sum(pattern, axis=0).astype(jnp.int32), jnp.zeros((1,), jnp.int32)])
    nonzero = per_column[old_slots]
    owner_loads = jnp.sum(nonzero, axis=1)
    leaving = nonzero[:, 0]
    coming = jnp.roll(nonzero[:, CSLOT - 1], -1)
    next_loads = jnp.roll(owner_loads, -1)
    gap_before = jnp.abs(owner_loads - next_loads)
    gap_after = jnp.abs(owner_loads - next_loads - 2 * leaving + 2 * coming)
    exchanged = (gap_after < gap_before) | forced_owner
    first_new = jnp.where(exchanged, jnp.roll(old_slots[:, CSLOT - 1], -1), old_slots[:, 0])
    last_new = jnp.where(jnp.roll(exchanged, 1), jnp.roll(old_slots[:, 0], 1), old_slots[:, CSLOT - 1])
    new_slots = old_slots.at[:, 0].set(first_new).at[:, CSLOT - 1].set(last_new)
    return (old_slots.astype(jnp.int32), new_slots.astype(jnp.int32))


def draw_block_mask(key, part):
    return draw_pattern(key)


def draw_old_columns(key, part):
    return draw_owners(key)[0]


def draw_new_columns(key, part):
    return draw_owners(key)[1]


def levels(own_key, extent, cuts, least, largest):
    gain = 1.0
    for axis_at, parts in cuts:
        draws = jax.random.uniform(jax.random.fold_in(jax.random.fold_in(own_key, 6), axis_at), (parts,), jnp.float32, least / len(cuts), largest / len(cuts))
        gain = gain * jnp.repeat(jnp.exp(draws), extent[axis_at] // parts).reshape((-1,) + (1,) * (len(extent) - 1 - axis_at))
    return gain


def normal_values(stream_key, dims, scale, bound, cuts=(), kind=jnp.bfloat16):
    values = jax.random.normal(stream_key, dims, jnp.float32) * scale
    if len(cuts) > 0:
        values = levels(stream_key, dims, cuts, -0.22, 0.18) * values
    return jnp.clip(values, min=-bound, max=bound).astype(kind)


def setup_inputs(seed: int = 0) -> dict:
    keys = jax.random.split(jax.random.key(seed), 9)
    return {
        "features": normal_values(keys[0], (TOKENS, D), 1.0, 6.0, ((0, 4),)),
        "hidden_grad": normal_values(keys[1], (TOKENS, SLOTS_ALL * BS), TOKENS ** -0.5, 0.125, ((0, 4), (1, 8))),
        "block_mask": draw_block_mask(jax.random.fold_in(keys[8], 71), 0),
        "old_columns": draw_old_columns(jax.random.fold_in(keys[8], 71), 0),
        "new_columns": draw_new_columns(jax.random.fold_in(keys[8], 71), 0),
        "weights": normal_values(keys[5], (N_TOK, SLOTS_ALL, KCAP, BS, BS), 0.05, 0.75, ((0, 4), (1, 8)), jnp.float32),
        "first_moment": normal_values(keys[6], (N_TOK, SLOTS_ALL, KCAP, BS, BS), 0.5, 6.0, ((0, 4), (1, 8)), jnp.float32),
        "second_moment": jnp.clip(jnp.exp(math.log(1.0) - 6.9077552 * jax.random.uniform(keys[7], (N_TOK, SLOTS_ALL, KCAP, BS, BS), jnp.float32) ** levels(keys[7], (N_TOK, SLOTS_ALL, KCAP, BS, BS), ((0, 4), (1, 8)), -0.2, 0.2)), 0.001, 1.0),
    }


beta_one = 0.9
beta_two = 0.95
learn_rate = 0.05
weight_decay = 0.1
adam_eps = 1e-08
adam_steps = 20.0

def block_rows(block_mask, columns, first_row, range_rows, capacity):
    total_cols = block_mask.shape[1]
    window = lax.dynamic_slice_in_dim(block_mask, first_row, range_rows, 0)
    selector = (columns[:, None] == jnp.arange(total_cols, dtype=jnp.int32)[None, :]).astype(jnp.int32)
    present = lax.optimization_barrier(jnp.sum(selector[:, None, :] * window[None, :, :], axis=2)).astype(jnp.int32)
    running = jnp.cumsum(present, axis=1).astype(jnp.int32)
    places = jnp.arange(capacity, dtype=jnp.int32)
    local_rows = jnp.arange(range_rows, dtype=jnp.int32)
    matches = (present[:, None, :] == 1) & (running[:, None, :] == places[None, :, None] + 1)
    row_ids = lax.optimization_barrier(jnp.sum(jnp.where(matches, local_rows[None, None, :], 0), axis=2)).astype(jnp.int32)
    usable = (running[:, -1:] > places[None, :]).astype(jnp.float32)
    return (row_ids, usable)

def adam_update(weights, moment_one, moment_two, gradient):
    first_new = beta_one * moment_one + (1.0 - beta_one) * gradient
    second_new = beta_two * moment_two + (1.0 - beta_two) * gradient * gradient
    fix_one = 1.0 - beta_one ** adam_steps
    fix_two = 1.0 - beta_two ** adam_steps
    update = first_new / fix_one / (jnp.sqrt(second_new / fix_two) + adam_eps)
    stepped = weights - learn_rate * (update + weight_decay * weights)
    return (stepped, first_new, second_new)

def reference(features, hidden_grad, block_mask, old_columns, new_columns, weights, first_moment, second_moment):
    old_flat = old_columns.reshape(-1)
    new_flat = new_columns.reshape(-1)
    token_blocks = features.reshape(TOKENS, NRB, BS)
    slot_ids = jnp.arange(SLOTS_ALL, dtype=jnp.int32)
    owner_ids = slot_ids // CSLOT
    position = slot_ids % CSLOT
    changed = new_flat != old_flat
    from_upper = (owner_ids + 1) % OWNERS * CSLOT + CSLOT - 1
    from_lower = (owner_ids + OWNERS - 1) % OWNERS * CSLOT
    source = jnp.where(changed & (position == 0), from_upper, jnp.where(changed & (position == CSLOT - 1), from_lower, slot_ids)).astype(jnp.int32)
    weight_list = []
    first_list = []
    second_list = []
    for range_index in range(NRB // RB_T):
        first_row = range_index * RB_T
        local_ids, used_old = block_rows(block_mask, old_flat, first_row, RB_T, KCAP)
        global_ids = (local_ids + first_row).astype(jnp.int32)

        def per_slot(packed):
            slot_rows, slot_used, slot_index = packed
            token_tiles = jnp.take(token_blocks, slot_rows, axis=1).astype(jnp.float32)
            column = lax.dynamic_slice_in_dim(hidden_grad, slot_index * BS, BS, 1).astype(jnp.float32)
            gradient = jnp.einsum('tki,tj->kij', token_tiles, column)
            return gradient * slot_used[:, None, None]
        gradients = lax.map(per_slot, (global_ids, used_old, slot_ids))
        stepped, first_new, second_new = adam_update(weights[range_index], first_moment[range_index], second_moment[range_index], gradients)
        unused_rows, used_new = block_rows(block_mask, new_flat, first_row, RB_T, KCAP)
        keep_mask = used_new[:, :, None, None]
        weight_list.append(jnp.take(stepped, source, axis=0) * keep_mask)
        first_list.append(jnp.take(first_new, source, axis=0) * keep_mask)
        second_list.append(jnp.take(second_new, source, axis=0) * keep_mask)
    return (jnp.stack(weight_list), jnp.stack(first_list), jnp.stack(second_list))
```

```python
import functools

import jax
import jax.numpy as jnp
from jax import lax
from jax.experimental import pallas as pl
from jax.experimental.pallas import tpu as pltpu
from jax.sharding import PartitionSpec as P

beta_one = 0.9
beta_two = 0.95
learn_rate = 0.05
weight_decay = 0.1
adam_eps = 1e-08
adam_steps = 20.0
fix_one = 1.0 - beta_one**adam_steps
fix_two = 1.0 - beta_two**adam_steps

PAIR = 2
CHUNKS = 3


def shifted(value, axis, steps):
    count = lax.axis_size(axis)
    return lax.ppermute(value, axis, [(i, (i + steps) % count) for i in range(count)])


def block_rows(block_mask, columns, first_row, range_rows, capacity):
    window = lax.dynamic_slice_in_dim(block_mask, first_row, range_rows, 0)
    total_cols = block_mask.shape[1]
    selector = (columns[:, None] == jnp.arange(total_cols, dtype=jnp.int32)[None, :]).astype(jnp.int32)
    present = jnp.sum(selector[:, None, :] * window[None, :, :], axis=2)
    local_rows = jnp.arange(range_rows, dtype=jnp.int32)
    upto = (local_rows[None, :] <= local_rows[:, None]).astype(jnp.int32)
    running = jnp.sum(present[:, None, :] * upto[None, :, :], axis=2)
    places = jnp.arange(capacity, dtype=jnp.int32)
    matches = (present[:, None, :] == 1) & (running[:, None, :] == places[None, :, None] + 1)
    row_ids = jnp.sum(jnp.where(matches, local_rows[None, None, :], 0), axis=2)
    return row_ids, jnp.sum(present, axis=1)


def kernel(slot_of, rows_ref, count_ref, mine_ref, other_ref, hidden_ref, w_ref, m_ref, v_ref, *rest):
    ow_ref, om_ref, ov_ref, dense = rest[-4:]
    ranges, half_rows, _ = mine_ref.shape
    capacity, width = w_ref.shape[1], w_ref.shape[3]
    tile = min(512, half_rows)
    for half, lhs_ref in enumerate((mine_ref, other_ref)):

        @pl.loop(0, half_rows // tile)
        def _(step):
            at = pl.multiple_of(step * tile, tile)
            total = jnp.dot(
                lhs_ref[0, pl.ds(at, tile), :], hidden_ref[0], preferred_element_type=jnp.float32
            )
            for t in range(1, ranges):
                total += jnp.dot(
                    lhs_ref[t, pl.ds(at, tile), :], hidden_ref[t], preferred_element_type=jnp.float32
                )
            dense[pl.ds(pl.multiple_of(half * half_rows + at, tile), tile), :] = total

    first_slot = slot_of(pl.program_id(0)) * PAIR
    for s in range(PAIR):
        count = count_ref[first_slot + s]

        @pl.loop(0, capacity)
        def _(j):
            used = j < count

            @pl.when(used)
            def _():
                row = pl.multiple_of(rows_ref[(first_slot + s) * capacity + j] * width, width)
                gradient = dense[pl.ds(row, width), s * width : (s + 1) * width]
                first = beta_one * m_ref[s, j] + (1.0 - beta_one) * gradient
                second = beta_two * v_ref[s, j] + (1.0 - beta_two) * gradient * gradient
                update = (first * (1.0 / fix_one)) / (jnp.sqrt(second * (1.0 / fix_two)) + adam_eps)
                old = w_ref[s, j]
                ow_ref[s, j] = old - learn_rate * (update + weight_decay * old)
                om_ref[s, j] = first
                ov_ref[s, j] = second

            @pl.when(jnp.logical_not(used))
            def _():
                zero = jnp.zeros((width, width), jnp.float32)
                ow_ref[s, j] = zero
                om_ref[s, j] = zero
                ov_ref[s, j] = zero


def run_chunk(pairs, src_of, dst_of, rows, counts, mine, other, hidden, state, previous, total_slots):
    ranges, half_rows, tok_rows = mine.shape
    capacity, width = state[0].shape[1], state[0].shape[3]
    whole = lambda i, *_: (0, 0, 0)
    lhs_spec = pl.BlockSpec(mine.shape, whole, pipeline_mode=pl.Buffered(1))
    block = (PAIR, capacity, width, width)
    state_spec = pl.BlockSpec(block, lambda i, *_: (src_of(i), 0, 0, 0))
    out_spec = pl.BlockSpec(block, lambda i, *_: (dst_of(i), 0, 0, 0))
    out = jax.ShapeDtypeStruct((total_slots,) + block[1:], jnp.float32)
    aliases = {8 + i: i for i in range(3)} if previous else {}
    return pl.pallas_call(
        functools.partial(kernel, dst_of),
        grid_spec=pltpu.PrefetchScalarGridSpec(
            num_scalar_prefetch=2,
            grid=(pairs,),
            in_specs=[lhs_spec, lhs_spec]
            + [pl.BlockSpec((ranges, tok_rows, PAIR * width), lambda i, *_: (0, 0, i))]
            + [state_spec] * 3
            + [pl.BlockSpec(memory_space=pl.ANY)] * len(previous),
            out_specs=[out_spec] * 3,
            scratch_shapes=[pltpu.VMEM((2 * half_rows, PAIR * width), jnp.float32)],
        ),
        out_shape=[out] * 3,
        input_output_aliases=aliases,
        compiler_params=pltpu.CompilerParams(vmem_limit_bytes=44 * 1024 * 1024),
        cost_estimate=pl.CostEstimate(
            flops=4 * pairs * half_rows * ranges * tok_rows * PAIR * width,
            bytes_accessed=pairs * 24 * PAIR * capacity * width * width + 2 * 2 * mine.size,
            transcendentals=0,
        ),
    )(rows, counts, mine, other, hidden, *state, *previous)


def body(features, hidden_grad, block_mask, old_columns, new_columns, weights, first_moment, second_moment):
    ranges, owners = lax.axis_size("tok"), lax.axis_size("blk")
    tok_index, owner_index = lax.axis_index("tok"), lax.axis_index("blk")
    slots, capacity, width = weights.shape[1:4]
    total_rows = block_mask.shape[0]
    range_rows = total_rows // ranges
    tok_rows = features.shape[0]
    last = slots - 1
    state = [x[0] for x in (weights, first_moment, second_moment)]
    pairs = slots // PAIR
    cols = PAIR * width

    def gathered(x):
        return lax.all_gather(x, "tok", axis=0, tiled=False)

    inner = max(pairs - 2, 0)
    bounds = sorted({inner * i // CHUNKS for i in range(CHUNKS + 1)})
    chunks = [(1 + a, 1 + b) for a, b in zip(bounds[:-1], bounds[1:])]
    inner_hidden = [gathered(hidden_grad[:, a * cols : b * cols]) for a, b in chunks]

    core = owner_index % 2
    by_range = features.reshape(tok_rows, ranges, 2, range_rows // 2 * width)
    half = lax.dynamic_index_in_dim(by_range, core, 2, keepdims=False)
    half = jnp.transpose(half, (1, 2, 0))
    mine = lax.all_to_all(half, "tok", 0, 0)
    other = lax.ppermute(mine, "blk", [(i, i ^ 1) for i in range(owners)])

    old_mine = lax.dynamic_index_in_dim(old_columns, owner_index, 0, keepdims=False)
    new_mine = lax.dynamic_index_in_dim(new_columns, owner_index, 0, keepdims=False)
    into_first = new_mine[0] != old_mine[0]
    into_last = new_mine[last] != old_mine[last]
    row_ids, counts = block_rows(block_mask, new_mine, tok_index * range_rows, range_rows, capacity)
    rows = (row_ids + core * (range_rows // 2)) % range_rows
    rows = rows.reshape(-1).astype(jnp.int32)

    ends = [hidden_grad[:, :width], hidden_grad[:, last * width :]]
    lower = [shifted(x, "blk", 1) for x in (ends[0], *(x[0] for x in state))]
    upper = [shifted(x, "blk", -1) for x in (ends[1], *(x[last] for x in state))]
    head = [jnp.where(into_first, u, x) for u, x in zip(upper, (ends[0], *(x[0] for x in state)))]
    tail = [jnp.where(into_last, l, x) for l, x in zip(lower, (ends[1], *(x[last] for x in state)))]
    if pairs > 1:
        h_parts = [head[0], hidden_grad[:, width:cols], hidden_grad[:, (last - 1) * width : last * width], tail[0]]
        s_parts = [
            jnp.concatenate([head[1 + i][None], x[1:PAIR], x[last - 1 : last], tail[1 + i][None]], axis=0)
            for i, x in enumerate(state)
        ]
    else:
        h_parts = [head[0], tail[0]]
        s_parts = [jnp.stack([head[1 + i], tail[1 + i]]) for i in range(3)]
    outer_hidden = gathered(jnp.concatenate(h_parts, axis=1))

    out = []
    for (a, b), hidden in zip(chunks, inner_hidden):
        place = functools.partial(lambda base, i: base + i, a)
        out = run_chunk(b - a, place, place, rows, counts, mine, other, hidden, state, out, slots)
    out = run_chunk(
        min(pairs, 2), lambda i: i, lambda i: i * (pairs - 1), rows, counts, mine, other, outer_hidden, s_parts, out, slots
    )
    return tuple(x[None] for x in out)


def solution(mesh):
    stored = P("tok", "blk", None, None, None)
    return jax.shard_map(
        body,
        mesh=mesh,
        in_specs=(P("tok", None), P("tok", "blk"), P(), P(), P(), stored, stored, stored),
        out_specs=(stored, stored, stored),
        check_vma=False,
    )
```

```python
import functools

import jax
import jax.numpy as jnp
from jax import lax
from jax.experimental import pallas as pl
from jax.experimental.pallas import tpu as pltpu
from jax.sharding import PartitionSpec as P

beta_one = 0.9
beta_two = 0.95
learn_rate = 0.05
weight_decay = 0.1
adam_eps = 1e-08
adam_steps = 20.0
fix_one = 1.0 - beta_one**adam_steps
fix_two = 1.0 - beta_two**adam_steps

PAIR = 2
INNER = ((6, False), (6, False))
OUTER_GATHER = False
OUTER_AT = 2


def shifted(value, axis, steps):
    count = lax.axis_size(axis)
    return lax.ppermute(value, axis, [(i, (i + steps) % count) for i in range(count)])


def block_rows(block_mask, columns, first_row, range_rows, capacity):
    window = lax.dynamic_slice_in_dim(block_mask, first_row, range_rows, 0)
    total_cols = block_mask.shape[1]
    selector = (columns[:, None] == jnp.arange(total_cols, dtype=jnp.int32)[None, :]).astype(jnp.int32)
    present = jnp.sum(selector[:, None, :] * window[None, :, :], axis=2)
    local_rows = jnp.arange(range_rows, dtype=jnp.int32)
    upto = (local_rows[None, :] <= local_rows[:, None]).astype(jnp.int32)
    running = jnp.sum(present[:, None, :] * upto[None, :, :], axis=2)
    places = jnp.arange(capacity, dtype=jnp.int32)
    matches = (present[:, None, :] == 1) & (running[:, None, :] == places[None, :, None] + 1)
    row_ids = jnp.sum(jnp.where(matches, local_rows[None, None, :], 0), axis=2)
    return row_ids, jnp.sum(present, axis=1)


def swapped(value, axis, distance):
    count = lax.axis_size(axis)
    return lax.ppermute(value, axis, [(i, i ^ distance) for i in range(count)])


def kernel(slot_of, ranges, terms, rows_ref, count_ref, *refs):
    mine, other = refs[:ranges], refs[ranges : 2 * ranges]
    sources = 1 + max(source for source, _, _, _ in terms)
    hidden = refs[2 * ranges : 2 * ranges + sources]
    w_ref, m_ref, v_ref = refs[2 * ranges + sources : 2 * ranges + sources + 3]
    ow_ref, om_ref, ov_ref, dense = refs[-4:]
    half_rows = mine[0].shape[0]
    capacity, width = w_ref.shape[1], w_ref.shape[3]
    tile = min(512, half_rows)
    me = count_ref[count_ref.shape[0] - 1]
    for half, lhs in enumerate((mine, other)):

        @pl.loop(0, half_rows // tile)
        def _(step):
            at = pl.multiple_of(step * tile, tile)
            total = None
            for source, d, low, high in terms:
                ref = hidden[source]
                rhs = ref[me ^ d] if len(ref.shape) == 3 else ref[...]
                part = jnp.dot(
                    lhs[d][pl.ds(at, tile), low:high], rhs, preferred_element_type=jnp.float32
                )
                total = part if total is None else total + part
            dense[pl.ds(pl.multiple_of(half * half_rows + at, tile), tile), :] = total

    first_slot = slot_of(pl.program_id(0)) * PAIR
    for s in range(PAIR):
        count = count_ref[first_slot + s]

        @pl.loop(0, capacity)
        def _(j):
            used = j < count

            @pl.when(used)
            def _():
                row = pl.multiple_of(rows_ref[(first_slot + s) * capacity + j] * width, width)
                gradient = dense[pl.ds(row, width), s * width : (s + 1) * width]
                first = beta_one * m_ref[s, j] + (1.0 - beta_one) * gradient
                second = beta_two * v_ref[s, j] + (1.0 - beta_two) * gradient * gradient
                update = (first * (1.0 / fix_one)) / (jnp.sqrt(second * (1.0 / fix_two)) + adam_eps)
                old = w_ref[s, j]
                ow_ref[s, j] = old - learn_rate * (update + weight_decay * old)
                om_ref[s, j] = first
                ov_ref[s, j] = second

            @pl.when(jnp.logical_not(used))
            def _():
                zero = jnp.zeros((width, width), jnp.float32)
                ow_ref[s, j] = zero
                om_ref[s, j] = zero
                ov_ref[s, j] = zero


def run_chunk(pairs, src_of, dst_of, rows, counts, lhs, hidden, state, previous, total_slots):
    ranges = len(lhs) // 2
    half_rows, tok_rows = lhs[0].shape
    capacity, width = state[0].shape[1], state[0].shape[3]
    terms, hidden_arrays, hidden_at = hidden
    lhs_specs = [pl.BlockSpec(x.shape, lambda i, *_: (0, 0), pipeline_mode=pl.Buffered(1)) for x in lhs]
    hidden_specs = []
    for x, at in zip(hidden_arrays, hidden_at):
        if x.ndim == 3:
            hidden_specs.append(pl.BlockSpec(x.shape[:2] + (PAIR * width,), lambda i, *_, at=at: (0, 0, at + i)))
        else:
            hidden_specs.append(pl.BlockSpec((x.shape[0], PAIR * width), lambda i, *_, at=at: (0, at + i)))
    block = (PAIR, capacity, width, width)
    state_spec = pl.BlockSpec(block, lambda i, *_: (src_of(i), 0, 0, 0))
    out_spec = pl.BlockSpec(block, lambda i, *_: (dst_of(i), 0, 0, 0))
    out = jax.ShapeDtypeStruct((total_slots,) + block[1:], jnp.float32)
    first_alias = 2 + len(lhs) + len(hidden_arrays) + 3
    return pl.pallas_call(
        functools.partial(kernel, dst_of, ranges, terms),
        grid_spec=pltpu.PrefetchScalarGridSpec(
            num_scalar_prefetch=2,
            grid=(pairs,),
            in_specs=lhs_specs + hidden_specs + [state_spec] * 3
            + [pl.BlockSpec(memory_space=pl.ANY)] * len(previous),
            out_specs=[out_spec] * 3,
            scratch_shapes=[pltpu.VMEM((2 * half_rows, PAIR * width), jnp.float32)],
        ),
        out_shape=[out] * 3,
        input_output_aliases={first_alias + i: i for i in range(len(previous))},
        compiler_params=pltpu.CompilerParams(vmem_limit_bytes=44 * 1024 * 1024),
        cost_estimate=pl.CostEstimate(
            flops=8 * pairs * half_rows * ranges * tok_rows * PAIR * width,
            bytes_accessed=pairs * 24 * PAIR * capacity * width * width + 4 * ranges * lhs[0].size,
            transcendentals=0,
        ),
    )(rows, counts, *lhs, *hidden_arrays, *state, *previous)


def behind(value, earlier):
    return lax.optimization_barrier((value, earlier))[0]


def everywhere(own, own_at, sent, gather, landed):
    ranges = lax.axis_size("tok")
    tokens = sent.shape[0]
    if gather:
        whole = lax.all_gather(sent, "tok", axis=0, tiled=False)
        return [(0, d, 0, tokens) for d in range(ranges)], [whole], [0]
    terms, arrays = [(0, 0, 0, tokens)], [own]
    if ranges == 4:
        one, two = swapped(sent, "tok", 1), swapped(sent, "tok", 2)
        landed.append((one, two))
        cut = tokens // 2
        low, high = swapped(two[:cut], "tok", 1), swapped(one[cut:], "tok", 2)
        arrays += [one, two, low, high]
        terms += [(1, 1, 0, tokens), (2, 2, 0, tokens), (3, 3, 0, cut), (4, 3, cut, tokens)]
    else:
        for d in range(1, ranges):
            arrays.append(swapped(sent, "tok", d))
            terms.append((d, d, 0, tokens))
    return terms, arrays, [own_at] + [0] * (len(arrays) - 1)


def body(features, hidden_grad, block_mask, old_columns, new_columns, weights, first_moment, second_moment):
    ranges = lax.axis_size("tok")
    tok_index, owner_index = lax.axis_index("tok"), lax.axis_index("blk")
    slots, capacity, width = weights.shape[1:4]
    range_rows = block_mask.shape[0] // ranges
    last = slots - 1
    state = [x[0] for x in (weights, first_moment, second_moment)]
    pairs = slots // PAIR
    cols = PAIR * width

    inner = max(pairs - 2, 0)
    shares = sum(n for n, _ in INNER)
    chunks, done, seen = [], 0, 0
    for share, gather in INNER:
        seen += share
        until = inner * seen // shares
        if until > done:
            chunks.append((1 + done, 1 + until, gather))
        done = until
    core = owner_index % 2
    half_cols = range_rows // 2 * width

    def rows_of(range_index, half):
        start = (range_index * 2 + half) * half_cols
        return lax.dynamic_slice_in_dim(features, start, half_cols, 1).T

    going = [rows_of(tok_index ^ d, core) for d in range(1, ranges)]
    mine = [rows_of(tok_index, core)] + [swapped(x, "tok", d + 1) for d, x in enumerate(going)]
    other = [rows_of(tok_index, 1 - core)] + [swapped(x, "blk", 1) for x in mine[1:]]
    lhs = mine + other

    landed = [going, mine[1:]]

    def sent_columns(own, own_at, sent, gather):
        sent = behind(sent, landed[-2])
        return everywhere(own, own_at, sent, gather, landed)

    inner_parts = [
        sent_columns(hidden_grad, a, hidden_grad[:, a * cols : b * cols], gather) for a, b, gather in chunks
    ]

    old_mine = lax.dynamic_index_in_dim(old_columns, owner_index, 0, keepdims=False)
    new_mine = lax.dynamic_index_in_dim(new_columns, owner_index, 0, keepdims=False)
    into_first = new_mine[0] != old_mine[0]
    into_last = new_mine[last] != old_mine[last]
    row_ids, counts = block_rows(block_mask, new_mine, tok_index * range_rows, range_rows, capacity)
    rows = (row_ids + core * (range_rows // 2)) % range_rows
    rows = rows.reshape(-1).astype(jnp.int32)
    counts = jnp.concatenate([counts, tok_index[None]]).astype(jnp.int32)

    h_first, h_last = hidden_grad[:, :width], hidden_grad[:, last * width :]
    s_first, s_last = jnp.stack([x[0] for x in state]), jnp.stack([x[last] for x in state])
    h_head = jnp.where(into_first, shifted(h_last, "blk", -1), h_first)
    h_tail = jnp.where(into_last, shifted(h_first, "blk", 1), h_last)
    s_head = jnp.where(into_first, shifted(s_last, "blk", -1), s_first)
    s_tail = jnp.where(into_last, shifted(s_first, "blk", 1), s_last)
    if pairs > 1:
        h_parts = [h_head, hidden_grad[:, width:cols], hidden_grad[:, (last - 1) * width : last * width], h_tail]
        s_outer = [
            jnp.concatenate([s_head[i][None], x[1:PAIR], x[last - 1 : last], s_tail[i][None]], axis=0)
            for i, x in enumerate(state)
        ]
    else:
        h_parts = [h_head, h_tail]
        s_outer = [jnp.stack([s_head[i], s_tail[i]]) for i in range(3)]
    h_outer = jnp.concatenate(h_parts, axis=1)
    outer_part = sent_columns(h_outer, 0, h_outer, OUTER_GATHER)

    jobs = []
    for (a, b, _), part in zip(chunks, inner_parts):
        place = functools.partial(lambda base, i: base + i, a)
        jobs.append((b - a, place, place, part, state))
    outer = (min(pairs, 2), lambda i: i, lambda i: i * (pairs - 1), outer_part, s_outer)
    jobs.insert(OUTER_AT, outer)
    out = []
    for count, src_of, dst_of, part, held in jobs:
        out = run_chunk(count, src_of, dst_of, rows, counts, lhs, part, held, out, slots)
    return tuple(x[None] for x in out)


def solution(mesh):
    stored = P("tok", "blk", None, None, None)
    return jax.shard_map(
        body,
        mesh=mesh,
        in_specs=(P("tok", None), P("tok", "blk"), P(), P(), P(), stored, stored, stored),
        out_specs=(stored, stored, stored),
        check_vma=False,
    )
```
